256 devices in a mesh: loop: 32 (over x_lo, z, core), col: 8 (over x_hi, y).
Axes of the slice: x: 4 (x_hi: 2, x_lo: 2; x = x_hi * 2 + x_lo), y: 4, z: 8, core: 2. Of those that a mesh axis runs over, the one named last changes fastest.
Arguments:
- tokens: bfloat16 [4096, 2048], P('loop', 'col'), may hold values from -6 to 6
- cotangent: bfloat16 [4096, 2048], P('loop', 'col'), may hold values from -6 to 6
- routes: int32 [4096, 8], P('loop'), may hold values from 0 to 63, all different within a row; in each aligned block of 128 rows (0 to 127, 128 to 255, ...) at most 24 rows name the same one
- route_weights: float32 [4096, 8], P('loop'), may hold values from 0.05 to 0.5
- w_gate: bfloat16 [64, 1536, 2048], P('loop', 'col'), may hold values from -0.125 to 0.125
- w_up: bfloat16 [64, 1536, 2048], P('loop', 'col'), may hold values from -0.125 to 0.125
- w_down: bfloat16 [64, 1536, 2048], P('loop', 'col'), may hold values from -0.15625 to 0.15625
Outputs:
- mixed: bfloat16 [4096, 2048], P('loop', 'col')
- grad_tokens: bfloat16 [4096, 2048], P('loop', 'col')
- grad_gate: bfloat16 [64, 1536, 2048], P('loop', 'col')
- grad_up: bfloat16 [64, 1536, 2048], P('loop', 'col')
- grad_down: bfloat16 [64, 1536, 2048], P('loop', 'col')
The draws below stay inside these ranges and needn't reach their ends.
Inputs may be any that keep to these rules, and one draw needn't show every extreme that they name: `routes`: each token names 8 different experts. In the 128 rows of one block, no expert is named by more than 24 tokens, a bound that some block reaches.
All inputs are finite; a program needn't handle non-finite values.
Results may differ from the reference program's by a relative error of at most 0.018.
Values may be sent and summed in bfloat16 or wider, within the bound.
No kernel may reach another device: no remote copies, remote signals or barrier semaphores. Data moves between devices by JAX's collectives and lax.ppermute only.
A program may use at most 128 MiB of HBM per device.

```python
import math
import jax
import jax.numpy as jnp
import numpy as np
from jax import lax

D = 2048
FF = 1536
TOP = 8
TOK_DEV = 128
EXPERTS = 64
CAP = 24
TOKENS = 4096
N_LOOP = 32
N_COL = 8


def steps_of(rng, shape, shards, least, largest):
    gain, own = 1.0, jax.random.fold_in(rng, 6)
    for position, shards_of in shards:
        steps = jnp.exp(jax.random.uniform(jax.random.fold_in(own, position), (shards_of,), jnp.float32, least / len(shards), largest / len(shards)))
        gain = gain * jnp.repeat(steps, shape[position] // shards_of).reshape([-1 if axis == position else 1 for axis in range(len(shape))])
    return gain


def deal_out(stream_key, own, number, rows, amount, top, reach, lean):
    order = jax.random.permutation(stream_key, amount)
    crowded, usual = shares(amount, rows * top, reach, lean, True), shares(amount, rows * top, reach, lean, False)
    places = jnp.arange(amount)

    def named(tallies, turn):
        used = int((tallies > 0).sum())
        fixed = max(1, used // 4)
        shifted = fixed + (places - fixed + turn * (used - fixed)) % max(1, amount - fixed)
        return jnp.zeros((amount,), jnp.int32).at[order[jnp.where(places < fixed, places, shifted)]].set(jnp.asarray(tallies, jnp.int32))

    tallies = jnp.where(number % 4 == 0, named(crowded, number // 4), named(usual, number - number // 4 - 1))
    mixed = jax.random.permutation(jax.random.fold_in(own, 3), amount)
    source_of, taker = mixed[0:amount // 2 * 2:2], mixed[1:amount // 2 * 2:2]
    margin = jnp.minimum(tallies[source_of] - 1, reach - tallies[taker]) // 2
    margin = jnp.where((source_of == order[0]) | (taker == order[0]) | (tallies[taker] == 0), 0, jnp.maximum(margin, 0))
    shifted = jax.random.randint(jax.random.fold_in(own, 4), (amount // 2,), 0, 1 << 20) % (margin + 1)
    tallies = tallies.at[source_of].add(-shifted).at[taker].add(shifted)
    labels = jnp.searchsorted(jnp.cumsum(tallies), jnp.arange(rows * top), side="right").astype(jnp.int32)
    grid = labels.reshape(top, rows).T
    grid = grid[jax.random.permutation(jax.random.fold_in(own, 1), rows)]
    turn = jax.random.randint(jax.random.fold_in(own, 2), (rows, 1), 0, top)
    return jnp.take_along_axis(grid, (jnp.arange(top)[None, :] + turn) % top, axis=1)


def shares(amount, total, reach, slope, full):
    portions = [(1 << 20) // math.isqrt(rank ** slope) + 1 for rank in range(1, amount + 1)]
    largest = reach if full else min(reach, max(-(-total // amount), total * portions[0] // sum(portions)))
    least = 1 if total - largest >= amount - 1 else 0
    counts, rest = [largest] + [least] * (amount - 1), total - largest - least * (amount - 1)
    while rest > 0:
        free = [i for i in range(1, amount) if counts[i] < largest] or [i for i in range(1, amount) if counts[i] < reach]
        pool, remaining = sum([portions[i] for i in free]), rest
        for i in free:
            addition = min(reach - counts[i], max(1, remaining * portions[i] // pool), rest)
            counts[i] = counts[i] + addition
            rest = rest - addition
    return np.array(counts)


def scatter_about(stream_key, dims, width, bound, cuts=(), kind=jnp.bfloat16):
    factor_of = steps_of(stream_key, dims, cuts, -0.22, 0.18) if cuts else 1.0
    array = jax.random.normal(stream_key, dims, jnp.float32) * width * factor_of
    return jnp.minimum(jnp.maximum(array, -bound), bound).astype(kind)


def setup_inputs(seed: int = 0) -> dict:
    arg_keys = jax.random.split(jax.random.key(seed), 8)
    tokens = scatter_about(arg_keys[0], (TOKENS, D), 1.0, 6.0, ((0, 32), (1, 8)))
    cotangent = scatter_about(arg_keys[1], (TOKENS, D), 1.0, 6.0, ((0, 32), (1, 8)))
    routes_keys = jax.random.split(jax.random.fold_in(arg_keys[2], 1), TOKENS // TOK_DEV)
    routes_turns = jax.random.permutation(jax.random.fold_in(arg_keys[2], 3), TOKENS // TOK_DEV)
    routes = jax.vmap(lambda own, number: deal_out(jax.random.fold_in(arg_keys[2], 2), own, number, TOK_DEV, EXPERTS, TOP, CAP, 2))(routes_keys, routes_turns).reshape((TOKENS, TOP))
    route_weights = jnp.clip(jnp.exp(math.log(0.5) - 2.3025851 * jax.random.uniform(arg_keys[3], (TOKENS, TOP), jnp.float32) ** steps_of(arg_keys[3], (TOKENS, TOP), ((0, 32),), -0.2, 0.2)), 0.05, 0.5)
    w_gate = scatter_about(arg_keys[4], (EXPERTS, FF, D), D ** -0.5, 0.125, ((0, 32), (1, 8)))
    w_up = scatter_about(arg_keys[5], (EXPERTS, FF, D), D ** -0.5, 0.125, ((0, 32), (1, 8)))
    w_down = scatter_about(arg_keys[6], (EXPERTS, FF, D), FF ** -0.5, 0.15625, ((0, 32), (1, 8)))
    return {"tokens": tokens, "cotangent": cotangent, "routes": routes, "route_weights": route_weights, "w_gate": w_gate, "w_up": w_up, "w_down": w_down}


def slot_table(route_block, expert_count, capacity):
    flat = route_block.reshape(-1).astype(jnp.int32)
    pairs = flat.shape[0]
    onehot = (flat[:, None] == jnp.arange(expert_count, dtype=jnp.int32)[None, :]).astype(jnp.int32)
    ranks = jnp.sum((jnp.cumsum(onehot, axis=0) - 1) * onehot, axis=1).astype(jnp.int32)
    pair_slot = (flat * capacity + ranks).astype(jnp.int32)
    source_pair = jnp.zeros((expert_count * capacity,), jnp.int32).at[pair_slot].set(jnp.arange(pairs, dtype=jnp.int32))
    filled = jnp.zeros((expert_count * capacity,), jnp.float32).at[pair_slot].set(1.0)
    return pair_slot, source_pair, filled


def group_sum(terms):
    rounded = lax.optimization_barrier(terms.astype(jnp.bfloat16))
    return jnp.sum(rounded.astype(jnp.float32), axis=0).astype(jnp.bfloat16)


def expert_pass(operands):
    rows_x, rows_g, gate_w, up_w, down_w = operands
    count = rows_x.shape[0]
    group_width = FF // N_COL
    gate_act = jnp.dot(rows_x, gate_w.T, preferred_element_type=jnp.float32)
    up_act = jnp.dot(rows_x, up_w.T, preferred_element_type=jnp.float32)
    sigmoid_gate = jax.nn.sigmoid(gate_act)
    hidden = (gate_act * sigmoid_gate * up_act).astype(jnp.bfloat16)
    hidden_groups = hidden.reshape(count, N_COL, group_width).transpose(1, 0, 2).astype(jnp.float32)
    down_groups = down_w.reshape(N_COL, group_width, D).astype(jnp.float32)
    expert_out = group_sum(jnp.einsum('crf,cfh->crh', hidden_groups, down_groups))
    dhid = jnp.dot(rows_g, down_w.T, preferred_element_type=jnp.float32)
    d_up = (dhid * gate_act * sigmoid_gate).astype(jnp.bfloat16)
    d_gate = (dhid * up_act * sigmoid_gate * (1.0 + gate_act * (1.0 - sigmoid_gate))).astype(jnp.bfloat16)
    grad_down = jnp.dot(hidden.T, rows_g, preferred_element_type=jnp.float32).astype(jnp.bfloat16)
    grad_gate = jnp.dot(d_gate.T, rows_x, preferred_element_type=jnp.float32).astype(jnp.bfloat16)
    grad_up = jnp.dot(d_up.T, rows_x, preferred_element_type=jnp.float32).astype(jnp.bfloat16)
    dgate_groups = d_gate.reshape(count, N_COL, group_width).transpose(1, 0, 2).astype(jnp.float32)
    dup_groups = d_up.reshape(count, N_COL, group_width).transpose(1, 0, 2).astype(jnp.float32)
    wgate_groups = gate_w.reshape(N_COL, group_width, D).astype(jnp.float32)
    wup_groups = up_w.reshape(N_COL, group_width, D).astype(jnp.float32)
    terms = jnp.einsum('crf,cfh->crh', dgate_groups, wgate_groups) + jnp.einsum('crf,cfh->crh', dup_groups, wup_groups)
    expert_dx = group_sum(terms)
    return expert_out, expert_dx, grad_gate, grad_up, grad_down


def pick_rows(table, index):
    return table[index]


def reference(tokens, cotangent, routes, route_weights, w_gate, w_up, w_down):
    blocks = N_LOOP
    pairs = TOK_DEV * TOP
    pair_slot, source_pair, filled = jax.vmap(lambda block: slot_table(block, EXPERTS, CAP))(routes.reshape(blocks, TOK_DEV, TOP))
    token_of_slot = (source_pair // TOP).astype(jnp.int32)
    weight_flat = route_weights.reshape(blocks, pairs)
    weight_slot = jax.vmap(pick_rows)(weight_flat, source_pair) * filled
    tokens_dev = tokens.reshape(blocks, TOK_DEV, D)
    cot_dev = cotangent.reshape(blocks, TOK_DEV, D)
    slot_mask = filled.astype(jnp.bfloat16)[:, :, None]
    rows_x = jax.vmap(pick_rows)(tokens_dev, token_of_slot) * slot_mask
    rows_g = (jax.vmap(pick_rows)(cot_dev, token_of_slot).astype(jnp.float32) * weight_slot[:, :, None]).astype(jnp.bfloat16)
    rows_x = rows_x.reshape(blocks, EXPERTS, CAP, D).transpose(1, 0, 2, 3).reshape(EXPERTS, blocks * CAP, D)
    rows_g = rows_g.reshape(blocks, EXPERTS, CAP, D).transpose(1, 0, 2, 3).reshape(EXPERTS, blocks * CAP, D)
    expert_out, expert_dx, grad_gate, grad_up, grad_down = lax.map(expert_pass, (rows_x, rows_g, w_gate, w_up, w_down))
    out_dev = expert_out.reshape(EXPERTS, blocks, CAP, D).transpose(1, 0, 2, 3).reshape(blocks, EXPERTS * CAP, D)
    dx_dev = expert_dx.reshape(EXPERTS, blocks, CAP, D).transpose(1, 0, 2, 3).reshape(blocks, EXPERTS * CAP, D)
    pair_out = jax.vmap(pick_rows)(out_dev, pair_slot).reshape(blocks, TOK_DEV, TOP, D)
    pair_dx = jax.vmap(pick_rows)(dx_dev, pair_slot).reshape(blocks, TOK_DEV, TOP, D)
    mixed = jnp.sum(pair_out.astype(jnp.float32) * route_weights.reshape(blocks, TOK_DEV, TOP, 1), axis=2)
    grad_tokens = jnp.sum(pair_dx.astype(jnp.float32), axis=2)
    mixed = mixed.reshape(TOKENS, D).astype(jnp.bfloat16)
    grad_tokens = grad_tokens.reshape(TOKENS, D).astype(jnp.bfloat16)
    return (mixed, grad_tokens, grad_gate, grad_up, grad_down)
```

```python
import functools

import jax
import jax.numpy as jnp
from jax import lax
from jax.experimental import pallas as pl
from jax.experimental.pallas import tpu as pltpu
from jax.sharding import PartitionSpec as P

TOP = 8
N_Y = 4
BF = jnp.bfloat16
F32 = jnp.float32
VMEM_LIMIT = 60 * 1024 * 1024
VMEM = pl.BlockSpec(memory_space=pltpu.VMEM)
SMEM = pl.BlockSpec(memory_space=pltpu.SMEM)


def params():
    return pltpu.CompilerParams(vmem_limit_bytes=VMEM_LIMIT)


def dot(a, b, dims=((1,), (0,)), precision=None):
    return lax.dot_general(a, b, (dims, ((), ())), precision=precision, preferred_element_type=F32)


def iota(shape, dim):
    return lax.broadcasted_iota(jnp.int32, shape, dim)


def dispatch_kernel(capacity, routes_ref, weights_ref, tok_ref, cot_ref, x_ref, g_ref):
    slots = x_ref.shape[0]
    toks = tok_ref.shape[0]
    experts = slots // capacity
    ids = iota((experts, toks), 0)
    named = jnp.zeros((experts, toks), F32)
    weight = jnp.zeros((experts, toks), F32)
    for k in range(TOP):
        hit = routes_ref[k : k + 1, :] == ids
        named = named + jnp.where(hit, 1.0, 0.0)
        weight = weight + jnp.where(hit, weights_ref[k : k + 1, :], 0.0)
    earlier = jnp.where(iota((toks, toks), 0) < iota((toks, toks), 1), 1.0, 0.0).astype(BF)
    rank = dot(named.astype(BF), earlier)
    rank = jnp.where(named > 0.0, rank, -1.0).astype(BF)
    slot = iota((slots, experts), 0)
    first = iota((slots, experts), 1) * capacity
    owner = jnp.where((slot >= first) & (slot < first + capacity), 1.0, 0.0)
    place = lax.rem(iota((slots, toks), 0), jnp.int32(capacity)).astype(F32)
    taken = dot(owner.astype(BF), rank) == place
    slot_weight = dot(owner, weight, precision=lax.Precision.HIGHEST)
    slot_weight = jnp.sum(jnp.where(taken, slot_weight, 0.0), axis=1, keepdims=True)
    pick = jnp.where(taken, 1.0, 0.0).astype(BF)
    x_ref[...] = dot(pick, tok_ref[...]).astype(BF)
    g_ref[...] = (dot(pick, cot_ref[...]) * slot_weight).astype(BF)


def dispatch(routes, weights, tokens, cotangent, experts, capacity):
    shape = jax.ShapeDtypeStruct((experts * capacity, tokens.shape[1]), BF)
    return pl.pallas_call(
        functools.partial(dispatch_kernel, capacity),
        out_shape=(shape, shape),
        in_specs=[VMEM] * 4,
        out_specs=(VMEM, VMEM),
        compiler_params=params(),
        name="dispatch",
    )(routes.T, weights.T, tokens, cotangent)


def combine_kernel(capacity, weighted, routes_ref, weights_ref, rows_ref, out_ref):
    slots = rows_ref.shape[0]
    toks = out_ref.shape[0]
    experts = slots // capacity
    ids = iota((toks, experts), 1)
    named = jnp.zeros((toks, experts), F32)
    weight = jnp.zeros((toks, experts), F32)
    for k in range(TOP):
        hit = routes_ref[:, k : k + 1] == ids
        named = named + jnp.where(hit, 1.0, 0.0)
        weight = weight + jnp.where(hit, weights_ref[:, k : k + 1], 0.0)
    earlier = jnp.where(iota((toks, toks), 1) < iota((toks, toks), 0), 1.0, 0.0).astype(BF)
    rank = dot(earlier, named.astype(BF))
    rank = jnp.where(named > 0.0, rank, -1.0).astype(BF)
    slot = iota((experts, slots), 1)
    first = iota((experts, slots), 0) * capacity
    owner = jnp.where((slot >= first) & (slot < first + capacity), 1.0, 0.0)
    place = lax.rem(iota((toks, slots), 1), jnp.int32(capacity)).astype(F32)
    taken = dot(rank, owner.astype(BF)) == place
    if weighted:
        slot_weight = dot(weight, owner, precision=lax.Precision.HIGHEST)
        slot_weight = jnp.where(taken, slot_weight, 0.0)
        high = slot_weight.astype(BF)
        rest = slot_weight - high.astype(F32)
        mid = rest.astype(BF)
        low = (rest - mid.astype(F32)).astype(BF)
        rows = rows_ref[...]
        total = dot(high, rows) + (dot(mid, rows) + dot(low, rows))
    else:
        total = dot(jnp.where(taken, 1.0, 0.0).astype(BF), rows_ref[...])
    out_ref[...] = total.astype(BF)


def combine(routes, weights, rows, capacity, weighted):
    return pl.pallas_call(
        functools.partial(combine_kernel, capacity, weighted),
        out_shape=jax.ShapeDtypeStruct((routes.shape[0], rows.shape[1]), BF),
        in_specs=[VMEM] * 3,
        out_specs=VMEM,
        compiler_params=params(),
        name="combine_out" if weighted else "combine_dx",
    )(routes, weights, rows)


def columns(c, dx, dy, width):
    xh, y = c // N_Y, lax.rem(c, N_Y)
    block = jnp.bitwise_xor(xh, dx) * N_Y + lax.rem(y + dy, N_Y)
    return pl.ds(pl.multiple_of(block * width, width), width)


RELS = [(dx, dy) for dx in range(2) for dy in range(N_Y)]
TILE = 256


def forward_kernel(n_exp, c_ref, *refs):
    n = n_exp * len(RELS)
    x = refs[:n]
    wg, wu, wd = refs[n : n + 3]
    gate_ref, up_ref, hid_ref = refs[n + 3 : n + 6]
    out = refs[n + 6 :]
    c = c_ref[0]
    rows, width = x[0].shape
    cols = [columns(c, dx, dy, width) for dx, dy in RELS]
    for e in range(n_exp):

        @pl.loop(0, rows // TILE)
        def _(i):
            here = pl.ds(pl.multiple_of(i * TILE, TILE), TILE)
            gate = jnp.zeros((TILE, wg.shape[1]), F32)
            up = jnp.zeros((TILE, wg.shape[1]), F32)
            for r, col in enumerate(cols):
                part = x[e * len(RELS) + r][here, :]
                gate = gate + dot(part, wg[e, :, col], ((1,), (1,)))
                up = up + dot(part, wu[e, :, col], ((1,), (1,)))
            s = jax.nn.sigmoid(gate)
            hidden = (gate * s * up).astype(BF)
            gate_ref[e, here, :] = gate
            up_ref[e, here, :] = up
            hid_ref[e, here, :] = hidden
            for r, col in enumerate(cols):
                out[e * len(RELS) + r][here, :] = dot(hidden, wd[e, :, col]).astype(BF)


def backward_kernel(n_exp, c_ref, *refs):
    n = n_exp * len(RELS)
    g = refs[:n]
    wg, wu, wd, gate_ref, up_ref = refs[n : n + 5]
    dgate_ref, dup_ref = refs[n + 5 : n + 7]
    out = refs[n + 7 :]
    c = c_ref[0]
    rows, width = g[0].shape
    cols = [columns(c, dx, dy, width) for dx, dy in RELS]
    for e in range(n_exp):

        @pl.loop(0, rows // TILE)
        def _(i):
            here = pl.ds(pl.multiple_of(i * TILE, TILE), TILE)
            dhid = jnp.zeros((TILE, wd.shape[1]), F32)
            for r, col in enumerate(cols):
                dhid = dhid + dot(g[e * len(RELS) + r][here, :], wd[e, :, col], ((1,), (1,)))
            gate, up = gate_ref[e, here, :], up_ref[e, here, :]
            s = jax.nn.sigmoid(gate)
            dup = (dhid * gate * s).astype(BF)
            dgate = (dhid * up * s * (1.0 + gate * (1.0 - s))).astype(BF)
            dup_ref[e, here, :] = dup
            dgate_ref[e, here, :] = dgate
            for r, col in enumerate(cols):
                part = dot(dgate, wg[e, :, col]) + dot(dup, wu[e, :, col])
                out[e * len(RELS) + r][here, :] = part.astype(BF)


def grads_kernel(n_exp, n_left, c_ref, *refs):
    n = n_exp * len(RELS)
    right = refs[:n]
    left = refs[n : n + n_left]
    out = refs[n + n_left :]
    c = c_ref[0]
    width = right[0].shape[1]
    cols = [columns(c, dx, dy, width) for dx, dy in RELS]
    for e in range(n_exp):
        for a, o in zip(left, out):
            at = a[e].T
            for r, col in enumerate(cols):
                o[e, :, col] = dot(at, right[e * len(RELS) + r][...]).astype(BF)


def grads(c, right, left, n_exp, wshape):
    shape = jax.ShapeDtypeStruct(wshape, BF)
    return pl.pallas_call(
        functools.partial(grads_kernel, n_exp, len(left)),
        out_shape=(shape,) * len(left),
        in_specs=[SMEM] + [VMEM] * (len(right) + len(left)),
        out_specs=(VMEM,) * len(left),
        compiler_params=params(),
        name="grads%d" % len(left),
    )(c, *right, *left)


def send(a, dx, dy):
    perm = [
        (x * N_Y + y, ((x + dx) % 2) * N_Y + (y + dy) % N_Y) for x in range(2) for y in range(N_Y)
    ]
    return lax.ppermute(a, "col", perm)


def gather_col(own, sg):
    got = {(0, 0): own}
    got[0, -sg] = send(own, 0, sg)
    got[0, sg] = send(own, 0, -sg)
    got[1, 0] = send(own, 1, 0)
    got[0, 2] = send(got[0, -sg], 0, sg)
    got[1, sg] = send(got[1, 0], 0, -sg)
    got[1, -sg] = send(got[0, -sg], 1, 0)
    got[1, 2] = send(got[1, -sg], 0, sg)
    got = {(dx, dy % N_Y): a for (dx, dy), a in got.items()}
    return [got[r] for r in RELS]


def add(*parts):
    return sum(p.astype(F32) for p in parts).astype(BF)


def scatter_col(parts, sg):
    part = {r: a for r, a in zip(RELS, parts)}
    p = lambda dx, dy: part[dx, dy % N_Y]
    far = send(p(1, 2), 0, -sg)
    two = send(p(0, 2), 0, -sg)
    side = send(p(1, sg), 0, sg)
    cross = send(add(p(1, -sg), far), 1, 0)
    plus = send(p(0, sg), 0, sg)
    over = send(add(p(1, 0), side), 1, 0)
    minus = send(add(p(0, -sg), two, cross), 0, -sg)
    return add(p(0, 0), plus, over, minus)


def shards(tokens, cotangent, routes, route_weights, w_gate, w_up, w_down):
    loop_size = lax.axis_size("loop")
    n_exp, units, feats = w_gate.shape
    experts = loop_size * n_exp
    toks, width = tokens.shape
    capacity = max(2, 3 * toks * TOP // (2 * experts))
    c = lax.axis_index("col").astype(jnp.int32).reshape(1)
    rows = loop_size * capacity

    send_x, send_g = dispatch(routes, route_weights, tokens, cotangent, experts, capacity)

    def to_experts(a):
        a = a.reshape(loop_size, n_exp, capacity, width)
        a = lax.all_to_all(a, "loop", split_axis=0, concat_axis=0, tiled=True)
        return [a[:, e].reshape(rows, width) for e in range(n_exp)]

    def to_tokens(parts):
        a = jnp.stack([p.reshape(loop_size, capacity, width) for p in parts], axis=1)
        a = lax.all_to_all(a, "loop", split_axis=0, concat_axis=0, tiled=True)
        return a.reshape(experts * capacity, width)

    sign = [1 if e % 2 == 0 else -1 for e in range(n_exp)]
    x_own = to_experts(send_x)
    g_own = to_experts(send_g)
    xs = sum([gather_col(x_own[e], sign[e]) for e in range(n_exp)], [])
    gs = sum([gather_col(g_own[e], sign[e]) for e in range(n_exp)], [])

    block = jax.ShapeDtypeStruct((rows, width), BF)
    act = jax.ShapeDtypeStruct((n_exp, rows, units), F32)
    act_bf = jax.ShapeDtypeStruct((n_exp, rows, units), BF)
    n = n_exp * len(RELS)
    gate, up, hidden, *out_parts = pl.pallas_call(
        functools.partial(forward_kernel, n_exp),
        out_shape=(act, act, act_bf) + (block,) * n,
        in_specs=[SMEM] + [VMEM] * (n + 3),
        out_specs=(VMEM,) * (n + 3),
        compiler_params=params(),
        name="forward",
    )(c, *xs, w_gate, w_up, w_down)
    nr = len(RELS)
    outs = [scatter_col(out_parts[e * nr : e * nr + nr], sign[e]) for e in range(n_exp)]

    d_gate, d_up, *dx_parts = pl.pallas_call(
        functools.partial(backward_kernel, n_exp),
        out_shape=(act_bf, act_bf) + (block,) * n,
        in_specs=[SMEM] + [VMEM] * (n + 5),
        out_specs=(VMEM,) * (n + 2),
        compiler_params=params(),
        name="backward",
    )(c, *gs, w_gate, w_up, w_down, gate, up)
    dxs = [scatter_col(dx_parts[e * nr : e * nr + nr], sign[e]) for e in range(n_exp)]

    (grad_down,) = grads(c, gs, [hidden], n_exp, w_gate.shape)
    grad_gate, grad_up = grads(c, xs, [d_gate, d_up], n_exp, w_gate.shape)

    mixed = combine(routes, route_weights, to_tokens(outs), capacity, True)
    grad_tokens = combine(routes, route_weights, to_tokens(dxs), capacity, False)
    return (mixed, grad_tokens, grad_gate, grad_up, grad_down)


def solution(mesh):
    wide = P("loop", "col")
    narrow = P("loop", None)
    weight = P("loop", "col", None)
    return jax.shard_map(
        shards,
        mesh=mesh,
        in_specs=(wide, wide, narrow, narrow, weight, weight, weight),
        out_specs=(wide, wide, weight, weight, weight),
        check_vma=False,
    )
```

```python
import functools

import jax
import jax.numpy as jnp
from jax import lax
from jax.experimental import pallas as pl
from jax.experimental.pallas import tpu as pltpu
from jax.sharding import PartitionSpec as P

TOP = 8
N_Y = 4
BF = jnp.bfloat16
F32 = jnp.float32
VMEM_LIMIT = 60 * 1024 * 1024
VMEM = pl.BlockSpec(memory_space=pltpu.VMEM)
SMEM = pl.BlockSpec(memory_space=pltpu.SMEM)


def params():
    return pltpu.CompilerParams(vmem_limit_bytes=VMEM_LIMIT)


def dot(a, b, dims=((1,), (0,)), precision=None):
    return lax.dot_general(a, b, (dims, ((), ())), precision=precision, preferred_element_type=F32)


def iota(shape, dim):
    return lax.broadcasted_iota(jnp.int32, shape, dim)


def dispatch_kernel(capacity, n_exp, e, routes_ref, weights_ref, tok_ref, cot_ref, out_ref):
    rows = out_ref.shape[0]
    toks = tok_ref.shape[0]
    owners = rows // (2 * capacity)
    ids = iota((owners, toks), 0) * n_exp + e
    named = jnp.zeros((owners, toks), F32)
    weight = jnp.zeros((owners, toks), F32)
    for k in range(TOP):
        hit = routes_ref[k : k + 1, :] == ids
        named = named + jnp.where(hit, 1.0, 0.0)
        weight = weight + jnp.where(hit, weights_ref[k : k + 1, :], 0.0)
    earlier = jnp.where(iota((toks, toks), 0) < iota((toks, toks), 1), 1.0, 0.0).astype(BF)
    rank = dot(named.astype(BF), earlier)
    rank = jnp.where(named > 0.0, rank, -1.0).astype(BF)
    row = iota((rows, owners), 0)
    first = iota((rows, owners), 1) * (2 * capacity)
    owner = jnp.where((row >= first) & (row < first + 2 * capacity), 1.0, 0.0)
    place = lax.rem(iota((rows, toks), 0), jnp.int32(capacity)).astype(F32)
    taken = dot(owner.astype(BF), rank) == place
    row_weight = dot(owner, weight, precision=lax.Precision.HIGHEST)
    row_weight = jnp.sum(jnp.where(taken, row_weight, 0.0), axis=1, keepdims=True)
    pick = jnp.where(taken, 1.0, 0.0).astype(BF)
    x = dot(pick, tok_ref[...])
    g = dot(pick, cot_ref[...]) * row_weight
    second = lax.rem(iota(out_ref.shape, 0), jnp.int32(2 * capacity)) >= capacity
    out_ref[...] = jnp.where(second, g, x).astype(BF)


def dispatch(e, n_exp, owners, capacity, routes, weights, tokens, cotangent):
    return pl.pallas_call(
        functools.partial(dispatch_kernel, capacity, n_exp, e),
        out_shape=jax.ShapeDtypeStruct((owners * 2 * capacity, tokens.shape[1]), BF),
        in_specs=[VMEM] * 4,
        out_specs=VMEM,
        compiler_params=params(),
        name="dispatch%d" % e,
    )(routes, weights, tokens, cotangent)


def choose_kernel(capacity, n_exp, e, routes_ref, weights_ref, high_ref, mid_ref, low_ref, pick_ref):
    toks, rows = pick_ref.shape
    owners = rows // (2 * capacity)
    row = iota((owners, rows), 1)
    first = iota((owners, rows), 0) * (2 * capacity)
    owner = jnp.where((row >= first) & (row < first + 2 * capacity), 1.0, 0.0)
    spot = iota((toks, rows), 1)
    place = lax.rem(spot, jnp.int32(capacity)).astype(F32)
    second = lax.rem(spot, jnp.int32(2 * capacity)) >= capacity
    earlier = jnp.where(iota((toks, toks), 1) < iota((toks, toks), 0), 1.0, 0.0).astype(BF)
    ids = iota((toks, owners), 1) * n_exp + e
    named = jnp.zeros((toks, owners), F32)
    weight = jnp.zeros((toks, owners), F32)
    for k in range(TOP):
        hit = routes_ref[:, k : k + 1] == ids
        named = named + jnp.where(hit, 1.0, 0.0)
        weight = weight + jnp.where(hit, weights_ref[:, k : k + 1], 0.0)
    rank = dot(earlier, named.astype(BF))
    rank = jnp.where(named > 0.0, rank, -1.0).astype(BF)
    taken = dot(rank, owner.astype(BF)) == place
    row_weight = dot(weight, owner, precision=lax.Precision.HIGHEST)
    row_weight = jnp.where(taken & jnp.logical_not(second), row_weight, 0.0)
    high = row_weight.astype(BF)
    rest = row_weight - high.astype(F32)
    mid = rest.astype(BF)
    high_ref[...] = high
    mid_ref[...] = mid
    low_ref[...] = (rest - mid.astype(F32)).astype(BF)
    pick_ref[...] = jnp.where(taken & second, 1.0, 0.0).astype(BF)


def choose(e, n_exp, rows, capacity, routes, weights):
    shape = jax.ShapeDtypeStruct((routes.shape[0], rows), BF)
    return pl.pallas_call(
        functools.partial(choose_kernel, capacity, n_exp, e),
        out_shape=(shape,) * 4,
        in_specs=[VMEM] * 2,
        out_specs=(VMEM,) * 4,
        compiler_params=params(),
        name="choose%d" % e,
    )(routes, weights)


def combine_kernel(n_before, high, mid, low, pick, rows_ref, *refs):
    before, (mixed_ref, grad_ref) = refs[:n_before], refs[-2:]
    vals = rows_ref[...]
    mixed = dot(high[...], vals) + (dot(mid[...], vals) + dot(low[...], vals))
    grad = dot(pick[...], vals)
    if n_before:
        mixed = mixed + before[0][...]
        grad = grad + before[1][...]
    mixed_ref[...] = mixed.astype(mixed_ref.dtype)
    grad_ref[...] = grad.astype(grad_ref.dtype)


def combine(e, choice, rows, before, held):
    shape = jax.ShapeDtypeStruct((choice[0].shape[0], rows.shape[1]), BF if before else F32)
    return pl.pallas_call(
        functools.partial(combine_kernel, len(before)),
        out_shape=(shape, shape),
        in_specs=[VMEM] * (5 + len(before)) + [pl.BlockSpec(memory_space=pl.ANY)] * len(held),
        out_specs=(VMEM, VMEM),
        compiler_params=params(),
        name="combine%d" % e,
    )(*choice, rows, *before, *held)


RELS = [(dx, dy) for dx in range(2) for dy in range(N_Y)]
NR = len(RELS)
TILE = 256


def columns(c, width):
    xh, y = c // N_Y, lax.rem(c, N_Y)
    cols = []
    for dx, dy in RELS:
        block = jnp.bitwise_xor(xh, dx) * N_Y + lax.rem(y + dy, N_Y)
        cols.append(pl.ds(pl.multiple_of(block * width, width), width))
    return cols


def expert_kernel(c_ref, *refs):
    x, g = refs[:NR], refs[NR : 2 * NR]
    wg, wu, wd = refs[2 * NR : 2 * NR + 3]
    refs = refs[2 * NR + 3 :]
    hid_ref, dgate_ref, dup_ref = refs[:3]
    out = refs[3:]
    cols = columns(c_ref[0], x[0].shape[1])
    zero = jnp.zeros((x[0].shape[0], wg.shape[1]), F32)
    gate, up, dhid = zero, zero, zero
    for r, col in enumerate(cols):
        gate = gate + dot(x[r][...], wg[0, :, col], ((1,), (1,)))
        up = up + dot(x[r][...], wu[0, :, col], ((1,), (1,)))
    s = jax.nn.sigmoid(gate)
    hidden = (gate * s * up).astype(BF)
    hid_ref[...] = hidden
    for r, col in enumerate(cols):
        out[r][0] = dot(hidden, wd[0, :, col]).astype(BF)
    for r, col in enumerate(cols):
        dhid = dhid + dot(g[r][...], wd[0, :, col], ((1,), (1,)))
    dup = (dhid * gate * s).astype(BF)
    dgate = (dhid * up * s * (1.0 + gate * (1.0 - s))).astype(BF)
    dup_ref[...] = dup
    dgate_ref[...] = dgate
    for r, col in enumerate(cols):
        out[r][1] = (dot(dgate, wg[0, :, col]) + dot(dup, wu[0, :, col])).astype(BF)


def expert_pass(e, c, blocks, w_gate, w_up, w_down):
    rows, width = blocks[0].shape[0] // 2, blocks[0].shape[1]
    _, units, feats = w_gate.shape
    steps = rows // TILE
    act = jax.ShapeDtypeStruct((rows, units), BF)
    part = jax.ShapeDtypeStruct((2, rows, width), BF)
    flops = 2 * rows * units * feats * 6 * 3
    moved = 2 * (4 * NR * rows * width + 3 * units * feats + 3 * rows * units) * 3
    act_spec = pl.BlockSpec((TILE, units), lambda i: (i, 0))
    return pl.pallas_call(
        expert_kernel,
        grid=(steps,),
        out_shape=(act,) * 3 + (part,) * NR,
        in_specs=[SMEM]
        + [pl.BlockSpec((TILE, width), lambda i: (i, 0))] * NR
        + [pl.BlockSpec((TILE, width), lambda i: (i + steps, 0))] * NR
        + [pl.BlockSpec((1, units, feats), lambda i: (e, 0, 0))] * 3,
        out_specs=(act_spec,) * 3 + (pl.BlockSpec((2, TILE, width), lambda i: (0, i, 0)),) * NR,
        compiler_params=params(),
        cost_estimate=pl.CostEstimate(flops=flops, bytes_accessed=moved, transcendentals=0),
        name="expert%d" % e,
    )(c, *blocks, *blocks, w_gate, w_up, w_down)


def grads_kernel(n_old, c_ref, *refs):
    blocks = refs[:NR]
    hid, dgate, dup = refs[NR : NR + 3]
    down_ref, gate_ref, up_ref = refs[NR + 3 + n_old :]
    rows = hid.shape[0]
    cols = columns(c_ref[0], blocks[0].shape[1])
    hid_t, dgate_t, dup_t = hid[...].T, dgate[...].T, dup[...].T
    for r, col in enumerate(cols):
        x, g = blocks[r][:rows, :], blocks[r][rows:, :]
        down_ref[0, :, col] = dot(hid_t, g).astype(BF)
        gate_ref[0, :, col] = dot(dgate_t, x).astype(BF)
        up_ref[0, :, col] = dot(dup_t, x).astype(BF)


def grads(e, c, blocks, acts, old, wshape):
    shape = jax.ShapeDtypeStruct(wshape, BF)
    rows, units = acts[0].shape
    feats = wshape[2]
    spec = pl.BlockSpec((1, units, feats), lambda i: (e, 0, 0))
    moved = 2 * (2 * rows * feats + 3 * rows * units + 3 * units * feats)
    return pl.pallas_call(
        functools.partial(grads_kernel, len(old)),
        grid=(1,),
        out_shape=(shape,) * 3,
        in_specs=[SMEM] + [VMEM] * (NR + 3) + [pl.BlockSpec(memory_space=pl.ANY)] * len(old),
        out_specs=(spec,) * 3,
        input_output_aliases={1 + NR + 3 + i: i for i in range(len(old))},
        compiler_params=params(),
        cost_estimate=pl.CostEstimate(
            flops=6 * rows * units * feats, bytes_accessed=moved, transcendentals=0
        ),
        name="grads%d" % e,
    )(c, *blocks, *acts, *old)


class Links:
    def __init__(self):
        self.held = []

    def after(self, a, *earlier):
        a, *kept = lax.optimization_barrier((a, *earlier))
        self.held.extend(kept)
        return a

    def send(self, a, dx, dy, *earlier):
        perm = [
            (x * N_Y + y, ((x + dx) % 2) * N_Y + (y + dy) % N_Y)
            for x in range(2)
            for y in range(N_Y)
        ]
        if earlier:
            a = self.after(a, *earlier)
        return lax.ppermute(a, "col", perm)


def add(*parts):
    return sum(p.astype(F32) for p in parts).astype(BF)


def shards(tokens, cotangent, routes, route_weights, w_gate, w_up, w_down):
    owners = lax.axis_size("loop")
    n_exp = w_gate.shape[0]
    toks, width = tokens.shape
    capacity = max(2, 3 * toks * TOP // (2 * owners * n_exp))
    c = lax.axis_index("col").astype(jnp.int32).reshape(1)
    routes_t, weights_t = routes.T, route_weights.T
    links = Links()

    def swap(a):
        return lax.all_to_all(a, "loop", split_axis=0, concat_axis=0, tiled=True)

    def arrive(e, wait=None):
        sent = dispatch(e, n_exp, owners, capacity, routes_t, weights_t, tokens, cotangent)
        own = swap(sent.reshape(owners, 2, capacity, width))
        if wait is not None:
            own = links.after(own, wait)
        return own.transpose(1, 0, 2, 3).reshape(2 * owners * capacity, width)

    def leave(total):
        total = total.reshape(2, owners, capacity, width)
        return swap(total.transpose(1, 0, 2, 3)).reshape(owners * 2 * capacity, width)

    def run(e, blocks):
        out = expert_pass(e, c, blocks, w_gate, w_up, w_down)
        return out[:3], out[3:]

    def steps(gen, n):
        for _ in range(n):
            last = next(gen)
        return last

    send, after = links.send, links.after
    p = lambda parts: dict(zip(RELS, parts))

    own0 = arrive(0)
    a1 = send(own0, 0, 1)
    a2 = send(own0, 0, -1)
    a3 = send(own0, 1, 0)
    a4 = send(a1, 0, 1)
    a5 = send(a3, 0, -1, a2)
    a6 = send(a1, 1, 0, a3)
    a7 = send(a6, 0, 1, a4)
    got = {(0, 0): own0, (0, 3): a1, (0, 1): a2, (1, 0): a3, (0, 2): a4, (1, 1): a5, (1, 3): a6, (1, 2): a7}
    blocks0 = [got[r] for r in RELS]

    own1 = arrive(1)
    b1 = send(own1, 0, -1, a5)
    b2 = send(own1, 0, 1, a7)
    b3 = send(own1, 1, 0, a6)
    acts0, parts0 = run(0, blocks0)
    b4 = send(b1, 0, -1)
    b5 = send(b3, 0, 1, b2)
    b6 = send(b1, 1, 0, b3)
    b7 = send(b6, 0, -1, b4)
    got = {(0, 0): own1, (0, 1): b1, (0, 3): b2, (1, 0): b3, (0, 2): b4, (1, 3): b5, (1, 1): b6, (1, 2): b7}
    blocks1 = [got[r] for r in RELS]

    q = p(parts0)
    r1 = send(q[1, 2], 0, -1, b7)
    r3 = send(q[1, 1], 0, 1, b5)
    acts1, parts1 = run(1, blocks1)
    gate1 = parts1[:1]
    t = p(parts1)
    r4 = send(add(q[1, 3], r1), 1, 0, b6, *gate1)
    r2 = send(q[0, 2], 0, -1, r1)
    r5 = send(q[0, 1], 0, 1, r3)
    r6 = send(add(q[1, 0], r3), 1, 0, r4)
    s1 = send(t[1, 2], 0, 1, r5)
    s3 = send(t[1, 3], 0, -1, r2)
    r7 = send(add(q[0, 3], r2, r4), 0, -1, r2)
    total0 = add(q[0, 0], r5, r6, r7)
    s2 = send(t[0, 2], 0, 1, s1)
    s4 = send(add(t[1, 1], s1), 1, 0, r6)
    s5 = send(t[0, 3], 0, -1, r7)
    s6 = send(add(t[1, 0], s3), 1, 0, r6)
    s7 = send(add(t[0, 1], s2, s4), 0, 1)
    total1 = add(t[0, 0], s5, s6, s7)
    back0 = leave(total0)
    back1 = leave(total1)

    acts0 = [after(acts0[0], total1), *acts0[1:]]
    acts1 = [after(acts1[0], total1), *acts1[1:]]
    old = grads(0, c, blocks0, acts0, (), w_gate.shape)
    grad_down, grad_gate, grad_up = grads(1, c, blocks1, acts1, old, w_gate.shape)
    rows = owners * 2 * capacity
    choice = [choose(e, n_exp, rows, capacity, routes, route_weights) for e in range(n_exp)]
    part = combine(0, choice[0], back0, (), ())
    mixed, grad_tokens = combine(1, choice[1], back1, part, links.held)
    return (mixed, grad_tokens, grad_gate, grad_up, grad_down)


def solution(mesh):
    wide = P("loop", "col")
    narrow = P("loop", None)
    weight = P("loop", "col", None)
    return jax.shard_map(
        shards,
        mesh=mesh,
        in_specs=(wide, wide, narrow, narrow, weight, weight, weight),
        out_specs=(wide, wide, weight, weight, weight),
        check_vma=False,
    )
```

```python
import functools

import jax
import jax.numpy as jnp
from jax import lax
from jax.experimental import pallas as pl
from jax.experimental.pallas import tpu as pltpu
from jax.sharding import PartitionSpec as P

TOP = 8
N_Y = 4
BF = jnp.bfloat16
F32 = jnp.float32
VMEM_LIMIT = 60 * 1024 * 1024
VMEM = pl.BlockSpec(memory_space=pltpu.VMEM)
SMEM = pl.BlockSpec(memory_space=pltpu.SMEM)


def params():
    return pltpu.CompilerParams(vmem_limit_bytes=VMEM_LIMIT)


def dot(a, b, dims=((1,), (0,)), precision=None):
    return lax.dot_general(a, b, (dims, ((), ())), precision=precision, preferred_element_type=F32)


def iota(shape, dim):
    return lax.broadcasted_iota(jnp.int32, shape, dim)


def dispatch_kernel(capacity, n_exp, e, routes_ref, weights_ref, tok_ref, cot_ref, out_ref):
    rows = out_ref.shape[0]
    toks = tok_ref.shape[0]
    owners = rows // (2 * capacity)
    ids = iota((owners, toks), 0) * n_exp + e
    named = jnp.zeros((owners, toks), F32)
    weight = jnp.zeros((owners, toks), F32)
    for k in range(TOP):
        hit = routes_ref[k : k + 1, :] == ids
        named = named + jnp.where(hit, 1.0, 0.0)
        weight = weight + jnp.where(hit, weights_ref[k : k + 1, :], 0.0)
    earlier = jnp.where(iota((toks, toks), 0) < iota((toks, toks), 1), 1.0, 0.0).astype(BF)
    rank = dot(named.astype(BF), earlier)
    rank = jnp.where(named > 0.0, rank, -1.0).astype(BF)
    row = iota((rows, owners), 0)
    first = iota((rows, owners), 1) * (2 * capacity)
    owner = jnp.where((row >= first) & (row < first + 2 * capacity), 1.0, 0.0)
    place = lax.rem(iota((rows, toks), 0), jnp.int32(capacity)).astype(F32)
    taken = dot(owner.astype(BF), rank) == place
    row_weight = dot(owner, weight, precision=lax.Precision.HIGHEST)
    row_weight = jnp.sum(jnp.where(taken, row_weight, 0.0), axis=1, keepdims=True)
    pick = jnp.where(taken, 1.0, 0.0).astype(BF)
    x = dot(pick, tok_ref[...])
    g = dot(pick, cot_ref[...]) * row_weight
    second = lax.rem(iota(out_ref.shape, 0), jnp.int32(2 * capacity)) >= capacity
    out_ref[...] = jnp.where(second, g, x).astype(BF)


def dispatch(e, n_exp, owners, capacity, routes, weights, tokens, cotangent):
    return pl.pallas_call(
        functools.partial(dispatch_kernel, capacity, n_exp, e),
        out_shape=jax.ShapeDtypeStruct((owners * 2 * capacity, tokens.shape[1]), BF),
        in_specs=[VMEM] * 4,
        out_specs=VMEM,
        compiler_params=params(),
        name="dispatch%d" % e,
    )(routes, weights, tokens, cotangent)


def choose_kernel(capacity, n_exp, e, routes_ref, weights_ref, high_ref, mid_ref, low_ref, pick_ref):
    toks, rows = pick_ref.shape
    owners = rows // (2 * capacity)
    row = iota((owners, rows), 1)
    first = iota((owners, rows), 0) * (2 * capacity)
    owner = jnp.where((row >= first) & (row < first + 2 * capacity), 1.0, 0.0)
    spot = iota((toks, rows), 1)
    place = lax.rem(spot, jnp.int32(capacity)).astype(F32)
    second = lax.rem(spot, jnp.int32(2 * capacity)) >= capacity
    earlier = jnp.where(iota((toks, toks), 1) < iota((toks, toks), 0), 1.0, 0.0).astype(BF)
    ids = iota((toks, owners), 1) * n_exp + e
    named = jnp.zeros((toks, owners), F32)
    weight = jnp.zeros((toks, owners), F32)
    for k in range(TOP):
        hit = routes_ref[:, k : k + 1] == ids
        named = named + jnp.where(hit, 1.0, 0.0)
        weight = weight + jnp.where(hit, weights_ref[:, k : k + 1], 0.0)
    rank = dot(earlier, named.astype(BF))
    rank = jnp.where(named > 0.0, rank, -1.0).astype(BF)
    taken = dot(rank, owner.astype(BF)) == place
    row_weight = dot(weight, owner, precision=lax.Precision.HIGHEST)
    row_weight = jnp.where(taken & jnp.logical_not(second), row_weight, 0.0)
    high = row_weight.astype(BF)
    rest = row_weight - high.astype(F32)
    mid = rest.astype(BF)
    high_ref[...] = high
    mid_ref[...] = mid
    low_ref[...] = (rest - mid.astype(F32)).astype(BF)
    pick_ref[...] = jnp.where(taken & second, 1.0, 0.0).astype(BF)


def choose(e, n_exp, rows, capacity, routes, weights):
    shape = jax.ShapeDtypeStruct((routes.shape[0], rows), BF)
    return pl.pallas_call(
        functools.partial(choose_kernel, capacity, n_exp, e),
        out_shape=(shape,) * 4,
        in_specs=[VMEM] * 2,
        out_specs=(VMEM,) * 4,
        compiler_params=params(),
        name="choose%d" % e,
    )(routes, weights)


def combine_kernel(n_before, high, mid, low, pick, rows_ref, *refs):
    before, (mixed_ref, grad_ref) = refs[:n_before], refs[-2:]
    vals = rows_ref[...]
    mixed = dot(high[...], vals) + (dot(mid[...], vals) + dot(low[...], vals))
    grad = dot(pick[...], vals)
    if n_before:
        mixed = mixed + before[0][...]
        grad = grad + before[1][...]
    mixed_ref[...] = mixed.astype(mixed_ref.dtype)
    grad_ref[...] = grad.astype(grad_ref.dtype)


def combine(e, choice, rows, before, held):
    shape = jax.ShapeDtypeStruct((choice[0].shape[0], rows.shape[1]), BF if before else F32)
    return pl.pallas_call(
        functools.partial(combine_kernel, len(before)),
        out_shape=(shape, shape),
        in_specs=[VMEM] * (5 + len(before)) + [pl.BlockSpec(memory_space=pl.ANY)] * len(held),
        out_specs=(VMEM, VMEM),
        compiler_params=params(),
        name="combine%d" % e,
    )(*choice, rows, *before, *held)


RELS = [(dx, dy) for dx in range(2) for dy in range(N_Y)]
NR = len(RELS)
TILE = 384


def columns(c, width):
    xh, y = c // N_Y, lax.rem(c, N_Y)
    cols = []
    for dx, dy in RELS:
        block = jnp.bitwise_xor(xh, dx) * N_Y + lax.rem(y + dy, N_Y)
        cols.append(pl.ds(pl.multiple_of(block * width, width), width))
    return cols


def expert_kernel(c_ref, *refs):
    x, g = refs[:NR], refs[NR : 2 * NR]
    wg, wu, wd = refs[2 * NR : 2 * NR + 3]
    refs = refs[2 * NR + 3 :]
    hid_ref, dgate_ref, dup_ref = refs[:3]
    out = refs[3:-2]
    all_x, all_g = refs[-2:]
    cols = columns(c_ref[0], x[0].shape[1])
    for r, col in enumerate(cols):
        all_x[:, col] = x[r][...]
        all_g[:, col] = g[r][...]
    gate = dot(all_x[...], wg[0], ((1,), (1,)))
    up = dot(all_x[...], wu[0], ((1,), (1,)))
    s = jax.nn.sigmoid(gate)
    hidden = (gate * s * up).astype(BF)
    hid_ref[...] = hidden
    for r, col in enumerate(cols):
        out[r][0] = dot(hidden, wd[0, :, col]).astype(BF)
    dhid = dot(all_g[...], wd[0], ((1,), (1,)))
    dup = (dhid * gate * s).astype(BF)
    dgate = (dhid * up * s * (1.0 + gate * (1.0 - s))).astype(BF)
    dup_ref[...] = dup
    dgate_ref[...] = dgate
    for r, col in enumerate(cols):
        out[r][1] = (dot(dgate, wg[0, :, col]) + dot(dup, wu[0, :, col])).astype(BF)


def expert_pass(e, c, blocks, w_gate, w_up, w_down):
    rows, width = blocks[0].shape[0] // 2, blocks[0].shape[1]
    _, units, feats = w_gate.shape
    steps = rows // TILE
    act = jax.ShapeDtypeStruct((rows, units), BF)
    part = jax.ShapeDtypeStruct((2, rows, width), BF)
    flops = 2 * rows * units * feats * 6 * 3
    moved = 2 * (4 * NR * rows * width + 3 * units * feats + 3 * rows * units) * 3
    act_spec = pl.BlockSpec((TILE, units), lambda i: (i, 0))
    return pl.pallas_call(
        expert_kernel,
        grid=(steps,),
        out_shape=(act,) * 3 + (part,) * NR,
        in_specs=[SMEM]
        + [pl.BlockSpec((TILE, width), lambda i: (i, 0))] * NR
        + [pl.BlockSpec((TILE, width), lambda i: (i + steps, 0))] * NR
        + [pl.BlockSpec((1, units, feats), lambda i: (e, 0, 0))] * 3,
        out_specs=(act_spec,) * 3 + (pl.BlockSpec((2, TILE, width), lambda i: (0, i, 0)),) * NR,
        scratch_shapes=[pltpu.VMEM((TILE, feats), BF)] * 2,
        compiler_params=params(),
        cost_estimate=pl.CostEstimate(flops=flops, bytes_accessed=moved, transcendentals=0),
        name="expert%d" % e,
    )(c, *blocks, *blocks, w_gate, w_up, w_down)


def grads_kernel(n_old, c_ref, *refs):
    blocks = refs[:NR]
    hid, dgate, dup = refs[NR : NR + 3]
    down_ref, gate_ref, up_ref = refs[NR + 3 + n_old :]
    rows = hid.shape[0]
    cols = columns(c_ref[0], blocks[0].shape[1])
    hid_t, dgate_t, dup_t = hid[...].T, dgate[...].T, dup[...].T
    for r, col in enumerate(cols):
        x, g = blocks[r][:rows, :], blocks[r][rows:, :]
        down_ref[0, :, col] = dot(hid_t, g).astype(BF)
        gate_ref[0, :, col] = dot(dgate_t, x).astype(BF)
        up_ref[0, :, col] = dot(dup_t, x).astype(BF)


def grads(e, c, blocks, acts, old, wshape):
    shape = jax.ShapeDtypeStruct(wshape, BF)
    rows, units = acts[0].shape
    feats = wshape[2]
    spec = pl.BlockSpec((1, units, feats), lambda i: (e, 0, 0))
    moved = 2 * (2 * rows * feats + 3 * rows * units + 3 * units * feats)
    return pl.pallas_call(
        functools.partial(grads_kernel, len(old)),
        grid=(1,),
        out_shape=(shape,) * 3,
        in_specs=[SMEM] + [VMEM] * (NR + 3) + [pl.BlockSpec(memory_space=pl.ANY)] * len(old),
        out_specs=(spec,) * 3,
        input_output_aliases={1 + NR + 3 + i: i for i in range(len(old))},
        compiler_params=params(),
        cost_estimate=pl.CostEstimate(
            flops=6 * rows * units * feats, bytes_accessed=moved, transcendentals=0
        ),
        name="grads%d" % e,
    )(c, *blocks, *acts, *old)


class Links:
    def __init__(self):
        self.held = []

    def after(self, a, *earlier):
        a, *kept = lax.optimization_barrier((a, *earlier))
        self.held.extend(kept)
        return a

    def send(self, a, dx, dy, *earlier):
        perm = [
            (x * N_Y + y, ((x + dx) % 2) * N_Y + (y + dy) % N_Y)
            for x in range(2)
            for y in range(N_Y)
        ]
        if earlier:
            a = self.after(a, *earlier)
        return lax.ppermute(a, "col", perm)


def add(*parts):
    return sum(p.astype(F32) for p in parts).astype(BF)


def shards(tokens, cotangent, routes, route_weights, w_gate, w_up, w_down):
    owners = lax.axis_size("loop")
    n_exp = w_gate.shape[0]
    toks, width = tokens.shape
    capacity = max(2, 3 * toks * TOP // (2 * owners * n_exp))
    c = lax.axis_index("col").astype(jnp.int32).reshape(1)
    routes_t, weights_t = routes.T, route_weights.T
    links = Links()

    def swap(a):
        return lax.all_to_all(a, "loop", split_axis=0, concat_axis=0, tiled=True)

    def arrive(e, wait=None):
        sent = dispatch(e, n_exp, owners, capacity, routes_t, weights_t, tokens, cotangent)
        own = swap(sent.reshape(owners, 2, capacity, width))
        if wait is not None:
            own = links.after(own, wait)
        return own.transpose(1, 0, 2, 3).reshape(2 * owners * capacity, width)

    def leave(total):
        total = total.reshape(2, owners, capacity, width)
        return swap(total.transpose(1, 0, 2, 3)).reshape(owners * 2 * capacity, width)

    def run(e, blocks):
        out = expert_pass(e, c, blocks, w_gate, w_up, w_down)
        return out[:3], out[3:]

    def steps(gen, n):
        for _ in range(n):
            last = next(gen)
        return last

    send, after = links.send, links.after
    p = lambda parts: dict(zip(RELS, parts))

    own0 = arrive(0)
    a1 = send(own0, 0, 1)
    a2 = send(own0, 0, -1)
    a3 = send(own0, 1, 0)
    a4 = send(a1, 0, 1)
    a5 = send(a3, 0, -1, a2)
    a6 = send(a1, 1, 0, a3)
    a7 = send(a6, 0, 1, a4)
    got = {(0, 0): own0, (0, 3): a1, (0, 1): a2, (1, 0): a3, (0, 2): a4, (1, 1): a5, (1, 3): a6, (1, 2): a7}
    blocks0 = [got[r] for r in RELS]

    own1 = arrive(1)
    b1 = send(own1, 0, -1, a5)
    b2 = send(own1, 0, 1, a7)
    b3 = send(own1, 1, 0, a6)
    acts0, parts0 = run(0, blocks0)
    b4 = send(b1, 0, -1)
    b5 = send(b3, 0, 1, b2)
    b6 = send(b1, 1, 0, b3)
    b7 = send(b6, 0, -1, b4)
    got = {(0, 0): own1, (0, 1): b1, (0, 3): b2, (1, 0): b3, (0, 2): b4, (1, 3): b5, (1, 1): b6, (1, 2): b7}
    blocks1 = [got[r] for r in RELS]

    q = p(parts0)
    r1 = send(q[1, 2], 0, -1, b7)
    r3 = send(q[1, 1], 0, 1, b5)
    acts1, parts1 = run(1, blocks1)
    gate1 = parts1[:1]
    t = p(parts1)
    r4 = send(add(q[1, 3], r1), 1, 0, b6, *gate1)
    r2 = send(q[0, 2], 0, -1, r1)
    r5 = send(q[0, 1], 0, 1, r3)
    r6 = send(add(q[1, 0], r3), 1, 0, r4)
    s1 = send(t[1, 2], 0, 1, r5)
    s3 = send(t[1, 3], 0, -1, r2)
    r7 = send(add(q[0, 3], r2, r4), 0, -1, r2)
    total0 = add(q[0, 0], r5, r6, r7)
    s2 = send(t[0, 2], 0, 1, s1)
    s4 = send(add(t[1, 1], s1), 1, 0, r6)
    s5 = send(t[0, 3], 0, -1, r7)
    s6 = send(add(t[1, 0], s3), 1, 0, r6)
    s7 = send(add(t[0, 1], s2, s4), 0, 1)
    total1 = add(t[0, 0], s5, s6, s7)
    back0 = leave(total0)
    back1 = leave(total1)

    acts0 = [after(acts0[0], total1), *acts0[1:]]
    acts1 = [after(acts1[0], total1), *acts1[1:]]
    old = grads(0, c, blocks0, acts0, (), w_gate.shape)
    grad_down, grad_gate, grad_up = grads(1, c, blocks1, acts1, old, w_gate.shape)
    rows = owners * 2 * capacity
    choice = [choose(e, n_exp, rows, capacity, routes, route_weights) for e in range(n_exp)]
    part = combine(0, choice[0], back0, (), ())
    mixed, grad_tokens = combine(1, choice[1], back1, part, links.held)
    return (mixed, grad_tokens, grad_gate, grad_up, grad_down)


def solution(mesh):
    wide = P("loop", "col")
    narrow = P("loop", None)
    weight = P("loop", "col", None)
    return jax.shard_map(
        shards,
        mesh=mesh,
        in_specs=(wide, wide, narrow, narrow, weight, weight, weight),
        out_specs=(wide, wide, weight, weight, weight),
        check_vma=False,
    )
```
